512 devices in a mesh: dp: 64 (over z_lo, y, core), mp: 8 (over x, z_hi).
Axes of the slice: x: 4, y: 8, z: 8 (z_hi: 2, z_lo: 4; z = z_hi * 4 + z_lo), core: 2. Of those that a mesh axis runs over, the one named last changes fastest.
Arguments:
- picture_encoder_features: bfloat16 [8192, 6144], P('dp', 'mp'), may hold values from -10 to 10
- caption_encoder_features: bfloat16 [8192, 2048], P('dp', 'mp'), may hold values from -10 to 10
- picture_head_matrix: bfloat16 [6144, 1024], P('mp'), may hold values from -2 to 2
- caption_head_matrix: bfloat16 [2048, 1024], P('mp'), may hold values from -2 to 2
- sharpness_factor: float32 [1], replicated, may hold values from 4 to 8
- offset_shift: float32 [1], replicated, may hold values from -2 to 0
Outputs:
- img_feat_grad: bfloat16 [8192, 6144], P('dp', 'mp')
- txt_feat_grad: bfloat16 [8192, 2048], P('dp', 'mp')
- w_img_grad: float32 [6144, 1024], P(('mp', 'dp'))
- w_txt_grad: float32 [2048, 1024], P(('mp', 'dp'))
The draws below stay inside these ranges and needn't reach their ends.
All inputs are finite; a program needn't handle non-finite values.
Results may differ from the reference program's by a relative error of at most 0.005.
Values may be sent and summed in bfloat16 or wider, within the bound.
A program may use at most 64 MiB of HBM per device.

```python
import math
import jax
import jax.numpy as jnp
from jax import lax

DI = 6144
DT = 2048
DE = 1024
PAIRS_DEV = 128
PAIRS = 8192
N_DP = 64
N_MP = 8


def shared_latent(key, mixing):
    base = jax.random.fold_in(key, 101)
    key_centers, key_cluster, key_sign, key_own = jax.random.split(base, 4)
    centers = jax.random.normal(key_centers, (4, DE), jnp.float32)
    cluster = jax.random.randint(key_cluster, (PAIRS,), 0, 4)
    signs = (2 * jax.random.randint(key_sign, (PAIRS,), 0, 2) - 1).astype(jnp.float32)
    own = jax.random.normal(key_own, (PAIRS, DE), jnp.float32)
    picked = jnp.take(centers, cluster, axis=0)
    return mixing * signs[:, None] * picked + math.sqrt(1.0 - mixing * mixing) * own


def owner_boost(width):
    row_owner = jnp.arange(PAIRS) // PAIRS_DEV
    column_block = jnp.arange(width) // (width // (N_MP * N_DP)) % N_DP
    matched = (row_owner[:, None] == column_block[None, :]).astype(jnp.float32)
    return 1.0 + 2.0 * matched


def tower_features(latent, noise, width):
    tiled = jnp.tile(latent, (1, width // DE))
    return jnp.clip(owner_boost(width) * (2.0 * tiled + noise), -10.0, 10.0)


def head_weight(noise, gain, width):
    row_index = jnp.arange(width) % DE
    diagonal = (row_index[:, None] == jnp.arange(DE)[None, :]).astype(jnp.float32)
    return (noise + math.sqrt(3.0 * DE) * gain * diagonal) / math.sqrt(width)


def draw_picture_encoder_features(key, part):
    latent = shared_latent(key, 0.84)
    key = jax.random.fold_in(key, 3)
    key_noise = jax.random.fold_in(key, 0)
    noise = jax.random.normal(key_noise, (PAIRS, DI), jnp.float32)
    return tower_features(latent, noise, DI).astype(jnp.bfloat16)


def draw_caption_encoder_features(key, part):
    latent = shared_latent(key, 0.84)
    key = jax.random.fold_in(key, 9)
    key_noise = jax.random.fold_in(key, 0)
    noise = jax.random.normal(key_noise, (PAIRS, DT), jnp.float32)
    return tower_features(latent, noise, DT).astype(jnp.bfloat16)


def draw_picture_head_matrix(key, part):
    key = jax.random.fold_in(key, 5)
    key_noise, key_gain = jax.random.split(key)
    noise = jnp.clip(jax.random.normal(key_noise, (DI, DE), jnp.float32), -4.0, 4.0)
    gain = jax.random.uniform(key_gain, (DI, DE), jnp.float32, 0.6, 1.4)
    return head_weight(noise, gain, DI).astype(jnp.bfloat16)


def draw_caption_head_matrix(key, part):
    key = jax.random.fold_in(key, 7)
    key_noise, key_gain = jax.random.split(key)
    noise = jnp.clip(jax.random.normal(key_noise, (DT, DE), jnp.float32), -4.0, 4.0)
    gain = jax.random.uniform(key_gain, (DT, DE), jnp.float32, 0.6, 1.4)
    return head_weight(noise, gain, DT).astype(jnp.bfloat16)


def setup_inputs(seed: int = 0) -> dict:
    streams_of = jax.random.split(jax.random.key(seed), 7)
    return {
        "picture_encoder_features": draw_picture_encoder_features(jax.random.fold_in(streams_of[6], 71), 0),
        "caption_encoder_features": draw_caption_encoder_features(jax.random.fold_in(streams_of[6], 71), 0),
        "picture_head_matrix": draw_picture_head_matrix(jax.random.fold_in(streams_of[6], 71), 0),
        "caption_head_matrix": draw_caption_head_matrix(jax.random.fold_in(streams_of[6], 71), 0),
        "sharpness_factor": jnp.clip(jax.random.uniform(streams_of[4], (1,), jnp.float32, 4.0, 8.0), 4.0, 8.0),
        "offset_shift": jnp.clip(jax.random.uniform(streams_of[5], (1,), jnp.float32, -2.0, 0.0), -2.0, 0.0),
    }


def unit_rows(values):
    scale = lax.rsqrt(lax.optimization_barrier(jnp.sum(values * values, axis=-1, keepdims=True)) + 1e-06)
    return (values * scale, scale)

def back_rows(emb, scale, grad):
    return scale * (grad - emb * lax.optimization_barrier(jnp.sum(emb * grad, axis=-1, keepdims=True)))

def reference(picture_encoder_features, caption_encoder_features, picture_head_matrix, caption_head_matrix, sharpness_factor, offset_shift):
    similarity_multiplier = sharpness_factor[0]
    offset_source_index = offset_shift[0]
    img_emb, img_scale = unit_rows(jnp.dot(picture_encoder_features, picture_head_matrix, preferred_element_type=jnp.float32))
    txt_emb, txt_scale = unit_rows(jnp.dot(caption_encoder_features, caption_head_matrix, preferred_element_type=jnp.float32))
    picture_unit_vectors = img_emb.astype(jnp.bfloat16)
    txt_unit = txt_emb.astype(jnp.bfloat16)
    total = PAIRS_DEV * N_DP
    width = 256
    count = total // width
    blocks = txt_unit.reshape(count, width, DE)
    starts = (jnp.arange(count) * width).astype(jnp.int32)
    img_rows = jnp.arange(total).astype(jnp.int32)

    def visit(carry, item):
        picture_running_total = carry
        tile_piece, start = item
        pair_similarities = similarity_multiplier * lax.dot_general(picture_unit_vectors, tile_piece, (((1,), (1,)), ((), ())), preferred_element_type=jnp.float32) + offset_source_index
        cols = start + jnp.arange(width).astype(jnp.int32)
        positive = img_rows[:, None] == cols[None, :]
        sign = jnp.where(positive, jnp.float32(1.0), jnp.float32(-1.0))
        multiplier = (-sign * jax.nn.sigmoid(-sign * pair_similarities)).astype(jnp.bfloat16)
        picture_running_total = picture_running_total + similarity_multiplier * jnp.dot(multiplier, tile_piece, preferred_element_type=jnp.float32)
        caption_derivative = similarity_multiplier * lax.dot_general(multiplier, picture_unit_vectors, (((0,), (0,)), ((), ())), preferred_element_type=jnp.float32)
        return (picture_running_total, caption_derivative)
    init = jnp.zeros((total, DE), jnp.float32)
    img_grad, txt_parts = lax.scan(visit, init, (blocks, starts))
    caption_derivative = txt_parts.reshape(total, DE)
    img_cot = back_rows(img_emb, img_scale, img_grad).astype(jnp.bfloat16)
    txt_cot = back_rows(txt_emb, txt_scale, caption_derivative).astype(jnp.bfloat16)
    img_feat_grad = lax.dot_general(img_cot, picture_head_matrix, (((1,), (1,)), ((), ())), preferred_element_type=jnp.float32).astype(jnp.bfloat16)
    txt_feat_grad = lax.dot_general(txt_cot, caption_head_matrix, (((1,), (1,)), ((), ())), preferred_element_type=jnp.float32).astype(jnp.bfloat16)
    w_img_grad = lax.dot_general(picture_encoder_features, img_cot, (((0,), (0,)), ((), ())), preferred_element_type=jnp.float32) / PAIRS_DEV
    w_txt_grad = lax.dot_general(caption_encoder_features, txt_cot, (((0,), (0,)), ((), ())), preferred_element_type=jnp.float32) / PAIRS_DEV
    return (img_feat_grad, txt_feat_grad, w_img_grad, w_txt_grad)
```

```python
import jax
import jax.numpy as jnp
from jax import lax
from jax.sharding import PartitionSpec as P


def unit_rows(values):
    scale = lax.rsqrt(jnp.sum(values * values, axis=-1, keepdims=True) + 1e-06)
    return (values * scale, scale)


def back_rows(emb, scale, grad):
    return scale * (grad - emb * jnp.sum(emb * grad, axis=-1, keepdims=True))


def dot(a, b, dims):
    return lax.dot_general(a, b, (dims, ((), ())), preferred_element_type=jnp.float32)


def shards(img_x, txt_x, img_w, txt_w, sharpness_factor, offset_shift):
    sharp = sharpness_factor[0]
    offset = offset_shift[0]
    groups = lax.axis_size("mp")
    member = lax.axis_index("mp")
    cycle = lax.axis_size("dp")
    place = lax.axis_index("dp")
    rows = img_x.shape[0]
    share = rows // groups
    width = img_w.shape[1]
    z_img = dot(img_x, img_w, ((1,), (0,))).reshape(groups, share, width)
    z_txt = dot(txt_x, txt_w, ((1,), (0,))).reshape(groups, share, width)
    z = lax.psum_scatter(
        jnp.concatenate([z_img, z_txt], axis=1), "mp", scatter_dimension=0, tiled=True
    )[0]
    emb, scale = unit_rows(z)
    unit = emb.astype(jnp.bfloat16)
    img_unit = lax.all_gather(unit[:share], "mp", axis=0, tiled=True)
    txt_unit = lax.all_gather(unit[share:], "dp", axis=0, tiled=True)
    logits = sharp * dot(txt_unit, img_unit, ((1,), (1,))) + offset
    t = jnp.arange(cycle * share)
    txt_index = (t // share) * rows + member * share + t % share
    img_index = place * rows + jnp.arange(rows)
    sign = jnp.where(txt_index[:, None] == img_index[None, :], 1.0, -1.0).astype(jnp.float32)
    coef = (-sign * jax.nn.sigmoid(-sign * logits)).astype(jnp.bfloat16)
    img_part = dot(coef, txt_unit, ((0,), (0,)))
    txt_part = dot(coef, img_unit, ((1,), (0,)))
    txt_grad = lax.psum_scatter(txt_part, "dp", scatter_dimension=0, tiled=True)
    img_grad = lax.psum_scatter(img_part, "mp", scatter_dimension=0, tiled=True)
    grad = sharp * jnp.concatenate([img_grad, txt_grad], axis=0)
    cot = back_rows(emb, scale, grad).astype(jnp.bfloat16)
    cots = lax.all_gather(cot, "mp", axis=0)
    img_cot = cots[:, :share].reshape(rows, width)
    txt_cot = cots[:, share:].reshape(rows, width)
    img_feat_grad = dot(img_cot, img_w, ((1,), (1,))).astype(jnp.bfloat16)
    txt_feat_grad = dot(txt_cot, txt_w, ((1,), (1,))).astype(jnp.bfloat16)
    w_img = (dot(img_x, img_cot, ((0,), (0,))) / rows).reshape(cycle, -1, width)
    w_txt = (dot(txt_x, txt_cot, ((0,), (0,))) / rows).reshape(cycle, -1, width)
    n_img = w_img.shape[1]
    w = lax.psum_scatter(
        jnp.concatenate([w_img, w_txt], axis=1), "dp", scatter_dimension=0, tiled=True
    )[0]
    return (img_feat_grad, txt_feat_grad, w[:n_img], w[n_img:])


def solution(mesh):
    placed = (P("dp", "mp"), P("dp", "mp"), P("mp", None), P("mp", None), P(), P())
    return jax.shard_map(
        shards,
        mesh=mesh,
        in_specs=placed,
        out_specs=(P("dp", "mp"), P("dp", "mp"), P(("mp", "dp"), None), P(("mp", "dp"), None)),
        check_vma=False,
    )
```
